32 devices in a mesh: tm: 8 (over z, x), mp: 4 (over y, core).
Axes of the slice: x: 2, y: 2, z: 4, core: 2. Of those that a mesh axis runs over, the one named last changes fastest.
Arguments:
- frames: bfloat16 [1536, 4096], P('mp', 'tm'), may hold values from -40 to 40
- norm_gain: float32 [1536], replicated, may hold values from 0.1 to 1.9
- w_qkv: bfloat16 [3, 1536, 1536], P(None, 'mp'), may hold values from -0.76546554 to 0.76546554
- w_out: bfloat16 [1536, 1536], P('mp'), may hold values from -0.15625 to 0.15625
- conv_kernel: float32 [31, 1536], P(None, 'mp'), may hold values from -1 to 1
- grad_out: bfloat16 [1536, 4096], P('mp', 'tm'), may hold values from -6 to 6
Outputs:
- block_out: bfloat16 [1536, 4096], P('mp', 'tm')
- grad_frames: bfloat16 [1536, 4096], P('mp', 'tm')
- grad_gain: float32 [1536], P('mp')
- grad_qkv: float32 [3, 1536, 1536], P(None, 'mp')
- grad_out_proj: float32 [1536, 1536], P('mp')
- grad_kernel: float32 [31, 1536], P(None, 'mp')
The draws below stay inside these ranges and needn't reach their ends.
All inputs are finite; a program needn't handle non-finite values.
Results may differ from the reference program's by a relative error of at most 0.023.
The reference program's roundings to bfloat16 on the way (of `normed`, `packed`, `attended`, `residual_sum`, `back_cast`, `grad_attn`, `grad_score` and `grad_packed`) count: a program that leaves them out, or rounds other values in their place, can miss the bound.
Values may be sent and summed in bfloat16 or wider, within the bound.
A program may use at most 128 MiB of HBM per device.

```python
import math
import jax
import jax.numpy as jnp
from jax import lax

D = 1536
HEADS = 24
HEAD_DIM = 64
KERNEL = 31
TOKENS = 4096


def draw_frames(key, part):
    first_key, second_key, third_key = jax.random.split(key, 3)
    entries = jax.random.truncated_normal(first_key, -4.0, 4.0, (TOKENS, D), jnp.float32)
    row_scale = jnp.exp(jax.random.uniform(second_key, (TOKENS, 1), jnp.float32, -0.8, 0.8))
    col_scale = jnp.exp(jax.random.uniform(third_key, (1, D), jnp.float32, -0.8, 0.8))
    return jnp.clip(entries * row_scale * col_scale, -40.0, 40.0).T.astype(jnp.bfloat16)


def draw_w_qkv(key, part):
    first_key, second_key = jax.random.split(key, 2)
    strength = jnp.exp(jax.random.uniform(second_key, (HEADS,), jnp.float32, -0.5, 0.3))
    column = jnp.repeat(strength, HEAD_DIM)
    entries = jax.random.truncated_normal(first_key, -4.0, 4.0, (3, HEADS * HEAD_DIM, D), jnp.float32)
    factors = jnp.stack([column, column, jnp.ones_like(column)])[:, :, None]
    return (entries * factors / math.sqrt(D)).astype(jnp.bfloat16)


def level_of(rng, dims, pieces, least, top_value):
    level, own = 1.0, jax.random.fold_in(rng, 6)
    for position, parts in pieces:
        heights = jnp.exp(jax.random.uniform(jax.random.fold_in(own, position), (parts,), jnp.float32, least / len(pieces), top_value / len(pieces)))
        level = level * jnp.repeat(heights, dims[position] // parts).reshape([-1 if axis == position else 1 for axis in range(len(dims))])
    return level


def gaussian(key, dims, width, reach, shards=(), held_as=jnp.bfloat16):
    gain = level_of(key, dims, shards, -0.22, 0.18) if shards else 1.0
    result = jax.random.normal(key, dims, jnp.float32) * width * gain
    return jnp.minimum(jnp.maximum(result, -reach), reach).astype(held_as)


def setup_inputs(seed: int = 0) -> dict:
    key_list = jax.random.split(jax.random.key(seed), 7)
    frames = draw_frames(jax.random.fold_in(key_list[6], 71), 0)
    norm_gain = jnp.clip(1.0 + 0.18 * jax.random.normal(key_list[1], (D,), jnp.float32), 0.1, 1.9)
    w_qkv = draw_w_qkv(jax.random.fold_in(key_list[6], 71), 0)
    w_out = gaussian(key_list[3], (HEADS * HEAD_DIM, D), (HEADS * HEAD_DIM) ** -0.5, 0.15625, ((0, 4),))
    conv_kernel = gaussian(key_list[4], (KERNEL, D), 0.2, 1.0, ((1, 4),), jnp.float32)
    grad_out = gaussian(key_list[5], (D, TOKENS), 1.0, 6.0, ((0, 4), (1, 8)))
    return dict(frames=frames, norm_gain=norm_gain, w_qkv=w_qkv, w_out=w_out, conv_kernel=conv_kernel, grad_out=grad_out)


def head_forward(operands):
    queries, key_rows, values = operands
    scores = jnp.dot(queries, key_rows.T, preferred_element_type=jnp.float32) * HEAD_DIM ** (-0.5)
    row_max = lax.optimization_barrier(jnp.max(scores, axis=1, keepdims=True))
    weights = jnp.exp(scores - row_max)
    row_total = lax.optimization_barrier(jnp.sum(weights, axis=1, keepdims=True))
    attended = jnp.dot(weights.astype(jnp.bfloat16), values, preferred_element_type=jnp.float32) / row_total
    return (attended.astype(jnp.bfloat16), (row_max + jnp.log(row_total))[:, 0])

def head_backward(operands):
    queries, key_rows, values, attended, grad_attn, logsum = operands
    score_scale = HEAD_DIM ** (-0.5)
    offset = lax.optimization_barrier(jnp.sum(grad_attn.astype(jnp.float32) * attended.astype(jnp.float32), axis=1, keepdims=True))
    scores = jnp.dot(queries, key_rows.T, preferred_element_type=jnp.float32) * score_scale
    probabilities = jnp.exp(scores - logsum[:, None])
    grad_prob = jnp.dot(grad_attn, values.T, preferred_element_type=jnp.float32)
    grad_score = (probabilities * (grad_prob - offset)).astype(jnp.bfloat16)
    grad_queries = jnp.dot(grad_score, key_rows, preferred_element_type=jnp.float32) * score_scale
    grad_keys = jnp.dot(grad_score.T, queries, preferred_element_type=jnp.float32) * score_scale
    grad_values = jnp.dot(probabilities.astype(jnp.bfloat16).T, grad_attn, preferred_element_type=jnp.float32)
    return (grad_queries, grad_keys, grad_values)

def reference(frames, norm_gain, w_qkv, w_out, conv_kernel, grad_out):
    inputs = frames.T.astype(jnp.float32)
    inverse = lax.rsqrt(lax.optimization_barrier(jnp.mean(inputs * inputs, axis=1, keepdims=True)) + 1e-06)
    normed = (inputs * inverse * norm_gain).astype(jnp.bfloat16)
    head_width = HEADS * HEAD_DIM
    qkv_rows = w_qkv.reshape(3 * head_width, D)
    packed = jnp.dot(normed, qkv_rows.T, preferred_element_type=jnp.float32).astype(jnp.bfloat16)
    packed = packed.reshape(TOKENS, 3, HEADS, HEAD_DIM).transpose(1, 2, 0, 3)
    attended, logsum = lax.map(head_forward, (packed[0], packed[1], packed[2]))
    attn_flat = attended.transpose(1, 0, 2).reshape(TOKENS, head_width)
    residual_sum = (inputs + jnp.dot(attn_flat, w_out, preferred_element_type=jnp.float32)).astype(jnp.bfloat16)
    half_width = KERNEL // 2
    resid = residual_sum.astype(jnp.float32)
    resid_pad = jnp.pad(resid, ((half_width, half_width), (0, 0)))
    upstream = grad_out.T.astype(jnp.float32)
    upstream_pad = jnp.pad(upstream, ((half_width, half_width), (0, 0)))
    conv_sum = jnp.zeros_like(resid)
    back_sum = upstream
    kernel_rows = []
    for tap_index in range(KERNEL):
        conv_sum = conv_sum + conv_kernel[tap_index] * resid_pad[tap_index:tap_index + TOKENS]
        mirror = 2 * half_width - tap_index
        back_sum = back_sum + conv_kernel[tap_index] * upstream_pad[mirror:mirror + TOKENS]
        kernel_rows.append(lax.optimization_barrier(jnp.sum(upstream * resid_pad[tap_index:tap_index + TOKENS], axis=0)))
    block_out = (resid + conv_sum).astype(jnp.bfloat16).T
    grad_kernel = jnp.stack(kernel_rows)
    back_cast = back_sum.astype(jnp.bfloat16)
    grad_out_proj = jnp.dot(attn_flat.T, back_cast, preferred_element_type=jnp.float32)
    grad_attn = jnp.dot(back_cast, w_out.T, preferred_element_type=jnp.float32).astype(jnp.bfloat16)
    grad_attn = grad_attn.reshape(TOKENS, HEADS, HEAD_DIM).transpose(1, 0, 2)
    grad_parts = lax.map(head_backward, (packed[0], packed[1], packed[2], attended, grad_attn, logsum))
    grad_packed = jnp.stack(grad_parts).transpose(2, 0, 1, 3).reshape(TOKENS, 3 * head_width).astype(jnp.bfloat16)
    grad_qkv = jnp.dot(grad_packed.T, normed, preferred_element_type=jnp.float32).reshape(3, head_width, D)
    grad_normed = jnp.dot(grad_packed, qkv_rows, preferred_element_type=jnp.float32)
    scaled = grad_normed * norm_gain
    grad_gain = lax.optimization_barrier(jnp.sum(grad_normed * inputs * inverse, axis=0))
    average = lax.optimization_barrier(jnp.mean(inputs * scaled, axis=1, keepdims=True))
    grad_frames = (back_sum + inverse * scaled - inputs * inverse ** 3 * average).astype(jnp.bfloat16).T
    return (block_out, grad_frames, grad_gain, grad_qkv, grad_out_proj, grad_kernel)
```

```python
import functools

import jax
import jax.numpy as jnp
from jax import lax
from jax.experimental import pallas as pl
from jax.experimental.pallas import tpu as pltpu
from jax.sharding import PartitionSpec as P

HEAD_DIM = 64
VMEM_LIMIT = 52 * 1024 * 1024
F32 = jnp.float32
BF16 = jnp.bfloat16


def dot(a, b):
    return jnp.dot(a, b, preferred_element_type=F32)


def greet(n, stride):
    tm = lax.axis_index("tm")
    lane, me = tm % stride, tm // stride
    barrier = pltpu.get_barrier_semaphore()
    for k in range(1, n):
        peer = ((me + k) % n) * stride + lane
        pl.semaphore_signal(
            barrier, inc=1, device_id={"tm": peer}, device_id_type=pl.DeviceIdType.MESH
        )
    pl.semaphore_wait(barrier, n - 1)
    return lane, me


def attend_kernel(n, stride, q_ref, kv_ref, o_ref, lse_ref, all_ref, m_ref, l_ref, acc_ref, send_sem, recv_sem):
    heads, _, rows = q_ref.shape
    chunk = min(512, rows)
    lane, me = greet(n, stride)

    def block_copy(k, h, slot):
        return pltpu.make_async_remote_copy(
            src_ref=kv_ref.at[h],
            dst_ref=all_ref.at[slot, h],
            send_sem=send_sem.at[k - 1, h],
            recv_sem=recv_sem.at[k - 1, h],
            device_id={"tm": ((me + n - k) % n) * stride + lane},
            device_id_type=pl.DeviceIdType.MESH,
        )

    for k in range(1, n):
        for h in range(heads):
            block_copy(k, h, me).start()
    all_ref[me] = kv_ref[...]
    m_ref[...] = jnp.full(m_ref.shape, -1e30, F32)
    l_ref[...] = jnp.zeros(l_ref.shape, F32)
    acc_ref[...] = jnp.zeros(acc_ref.shape, F32)

    def visit(slot, h):
        q = q_ref[h]
        q_pad = jnp.concatenate([q, jnp.zeros_like(q)], axis=0)
        for c in range(rows // chunk):
            kv_t = all_ref[slot, h, :, c * chunk : (c + 1) * chunk]
            scores = dot(kv_t.T, q_pad)
            old = m_ref[h]
            new = jnp.maximum(old, jnp.max(scores, axis=0, keepdims=True))
            weights = jnp.exp(scores - new)
            factor = jnp.exp(old - new)
            m_ref[h] = new
            l_ref[h] = l_ref[h] * factor + jnp.sum(weights, axis=0, keepdims=True)
            acc_ref[h] = acc_ref[h] * factor + dot(kv_t[HEAD_DIM:], weights.astype(BF16))

    def step(i, carry):
        k, h = i // heads, i % heads

        @pl.when(k > 0)
        def _():
            block_copy(k, h, (me + k) % n).wait_recv()

        visit((me + k) % n, h)
        return carry

    lax.fori_loop(0, n * heads, step, 0)
    o_ref[...] = (acc_ref[...] / l_ref[...]).astype(BF16)
    lse_ref[...] = m_ref[...] + jnp.log(l_ref[...])
    for k in range(1, n):
        for h in range(heads):
            block_copy(k, h, me).wait_send()


def attend(n, stride, q, kv):
    heads, _, rows = q.shape
    vmem = pl.BlockSpec(memory_space=pltpu.VMEM)
    work = n * heads * rows * rows
    return pl.pallas_call(
        functools.partial(attend_kernel, n, stride),
        out_shape=(
            jax.ShapeDtypeStruct(q.shape, BF16),
            jax.ShapeDtypeStruct((heads, 1, rows), F32),
            jax.ShapeDtypeStruct((n, *kv.shape), BF16),
        ),
        in_specs=[vmem] * 2,
        out_specs=(vmem,) * 3,
        scratch_shapes=[
            pltpu.VMEM((heads, 1, rows), F32),
            pltpu.VMEM((heads, 1, rows), F32),
            pltpu.VMEM((heads, HEAD_DIM, rows), F32),
            pltpu.SemaphoreType.DMA((n - 1, heads)),
            pltpu.SemaphoreType.DMA((n - 1, heads)),
        ],
        cost_estimate=pl.CostEstimate(flops=work * 4 * HEAD_DIM, bytes_accessed=8 * kv.size * n, transcendentals=work),
        compiler_params=pltpu.CompilerParams(collective_id=0, has_side_effects=True, vmem_limit_bytes=VMEM_LIMIT),
        name="attend",
    )(q, kv)


def attend_grad_kernel(
    n, stride, q_ref, all_ref, up_ref, lse_ref, off_ref,
    dq_ref, dkv_ref, q_pad, up_pad, q_rows, up_rows, dq_acc, own, out_buf, in_buf, send_sem, recv_sem,
):
    heads, _, rows = q_ref.shape
    chunk = min(512, rows)
    lane, me = greet(n, stride)
    dq_acc[...] = jnp.zeros(dq_acc.shape, F32)

    def prepare(h, carry):
        q, up = q_ref[h], up_ref[h]
        blank = jnp.zeros_like(q)
        low, high = jnp.concatenate([q, blank], axis=0), jnp.concatenate([blank, up], axis=0)
        q_pad[h] = low
        up_pad[h] = high
        q_rows[h] = low.T
        up_rows[h] = high.T
        return carry

    lax.fori_loop(0, heads, prepare, 0)

    def visit(slot, h, store):
        for c in range(rows // chunk):
            kv_t = all_ref[slot, h, :, c * chunk : (c + 1) * chunk]
            kv = kv_t.T
            probs = jnp.exp(dot(kv, q_pad[h]) - lse_ref[h])
            grads = (probs * (dot(kv, up_pad[h]) - off_ref[h])).astype(BF16)
            dq_acc[h] = dq_acc[h] + dot(kv_t[:HEAD_DIM], grads)
            store(c, dot(grads, q_rows[h]) + dot(probs.astype(BF16), up_rows[h]))

    def sum_copy(k, h):
        return pltpu.make_async_remote_copy(
            src_ref=out_buf.at[k - 1, h],
            dst_ref=in_buf.at[k - 1, h],
            send_sem=send_sem.at[k - 1, h],
            recv_sem=recv_sem.at[k - 1, h],
            device_id={"tm": ((me + k) % n) * stride + lane},
            device_id_type=pl.DeviceIdType.MESH,
        )

    def far(i, carry):
        k, h = i // heads + 1, i % heads

        def store(c, block):
            out_buf[k - 1, h, c * chunk : (c + 1) * chunk, :] = block.astype(BF16)

        visit((me + k) % n, h, store)
        sum_copy(k, h).start()
        return carry

    lax.fori_loop(0, (n - 1) * heads, far, 0)

    def near(h, carry):
        def store(c, block):
            own[h, c * chunk : (c + 1) * chunk, :] = block

        visit(me, h, store)
        return carry

    lax.fori_loop(0, heads, near, 0)
    dq_ref[...] = (dq_acc[...] * HEAD_DIM ** (-0.5)).astype(BF16)

    def finish(h, carry):
        total = own[h]
        for k in range(1, n):
            sum_copy(k, h).wait_recv()
            total = total + in_buf[k - 1, h].astype(F32)
        dkv_ref[h] = total.T.astype(BF16)
        for k in range(1, n):
            sum_copy(k, h).wait_send()
        return carry

    lax.fori_loop(0, heads, finish, 0)


def attend_grad(n, stride, q, kv_all, up, lse, off):
    heads, _, rows = q.shape
    vmem = pl.BlockSpec(memory_space=pltpu.VMEM)
    work = n * heads * rows * rows
    wide = 2 * HEAD_DIM
    return pl.pallas_call(
        functools.partial(attend_grad_kernel, n, stride),
        out_shape=(
            jax.ShapeDtypeStruct(q.shape, BF16),
            jax.ShapeDtypeStruct((heads, wide, rows), BF16),
        ),
        in_specs=[vmem] * 5,
        out_specs=(vmem,) * 2,
        scratch_shapes=[
            pltpu.VMEM((heads, wide, rows), BF16),
            pltpu.VMEM((heads, wide, rows), BF16),
            pltpu.VMEM((heads, rows, wide), BF16),
            pltpu.VMEM((heads, rows, wide), BF16),
            pltpu.VMEM((heads, HEAD_DIM, rows), F32),
            pltpu.VMEM((heads, rows, wide), F32),
            pltpu.VMEM((n - 1, heads, rows, wide), BF16),
            pltpu.VMEM((n - 1, heads, rows, wide), BF16),
            pltpu.SemaphoreType.DMA((n - 1, heads)),
            pltpu.SemaphoreType.DMA((n - 1, heads)),
        ],
        cost_estimate=pl.CostEstimate(flops=work * 10 * HEAD_DIM, bytes_accessed=8 * kv_all.size, transcendentals=work),
        compiler_params=pltpu.CompilerParams(collective_id=1, has_side_effects=True, vmem_limit_bytes=VMEM_LIMIT),
        name="attend_grad",
    )(q, kv_all, up, lse, off)


def swap(block):
    count = lax.axis_size("tm")
    return lax.ppermute(block, "tm", [(i, i ^ 1) for i in range(count)])


def halves(block):
    low, high = jnp.split(block, 2, axis=0)
    odd = lax.axis_index("tm") % 2 == 1
    return jnp.where(odd, high, low), jnp.where(odd, low, high)


def to_heads(block):
    keep, give = halves(block)
    return jnp.concatenate([keep, swap(give)], axis=2)


def to_rows(block):
    keep, give = jnp.split(block, 2, axis=2)
    got = swap(give)
    odd = lax.axis_index("tm") % 2 == 1
    return jnp.concatenate([jnp.where(odd, got, keep), jnp.where(odd, keep, got)], axis=0)


def with_halo(cells, width):
    count = lax.axis_size("tm")
    ends = count - 1
    return jnp.concatenate(
        [
            lax.ppermute(cells[:, -width:], "tm", [(i, i + 1) for i in range(ends)]),
            cells,
            lax.ppermute(cells[:, :width], "tm", [(i + 1, i) for i in range(ends)]),
        ],
        axis=1,
    )


def shards(frames, norm_gain, w_qkv, w_out, conv_kernel, grad_out):
    own_width, row_count = frames.shape
    head_cols, width = w_qkv.shape[1:]
    heads = head_cols // HEAD_DIM
    tm = lax.axis_size("tm")
    stride = 2 if heads % 2 == 0 and tm % 2 == 0 else 1
    n = tm // stride
    taps = conv_kernel.shape[0]
    half = taps // 2

    upstream = grad_out.astype(F32)
    upstream_pad = with_halo(grad_out, half).astype(F32)
    back_sum = upstream
    for tap in range(taps):
        mirror = 2 * half - tap
        back_sum = back_sum + conv_kernel[tap][:, None] * upstream_pad[:, mirror : mirror + row_count]
    back_cast = back_sum.astype(BF16)

    gathered = lax.all_gather(frames, "mp", axis=0, tiled=True)
    inputs = gathered.astype(F32)
    inverse = lax.rsqrt(jnp.mean(inputs * inputs, axis=0, keepdims=True) + 1e-06)
    normed = (inputs * inverse * norm_gain[:, None]).astype(BF16)
    qkv_rows = w_qkv.reshape(3 * head_cols, width)
    packed = dot(qkv_rows, normed).astype(BF16).reshape(3, heads, HEAD_DIM, row_count)
    merged = packed.transpose(1, 0, 2, 3).reshape(heads, 3 * HEAD_DIM, row_count)
    if stride == 2:
        merged = to_heads(merged)
    q = merged[:, :HEAD_DIM] * jnp.asarray(HEAD_DIM ** (-0.5), BF16)
    attended_heads, lse, kv_all = attend(n, stride, q, merged[:, HEAD_DIM:])
    back_full = lax.all_gather(back_cast, "mp", axis=0, tiled=True)
    grad_attn = dot(w_out, back_full).astype(BF16).reshape(heads, HEAD_DIM, row_count)
    if stride == 2:
        attended = to_rows(attended_heads)
        up = to_heads(grad_attn)
    else:
        attended, up = attended_heads, grad_attn
    off = jnp.sum(up.astype(F32) * attended_heads.astype(F32), axis=1, keepdims=True)
    dq, dkv = attend_grad(n, stride, q, kv_all, up, lse, off)

    attn = attended.reshape(head_cols, row_count)
    out_proj_part = jnp.einsum("ct,dt->cd", attn, back_full, preferred_element_type=F32)
    projected = jnp.einsum("cd,ct->dt", w_out, attn, preferred_element_type=F32)
    mixed = lax.psum_scatter(projected.astype(BF16), "mp", scatter_dimension=0, tiled=True)
    residual_sum = (frames.astype(F32) + mixed.astype(F32)).astype(BF16)
    resid_pad = with_halo(residual_sum, half).astype(F32)
    resid = residual_sum.astype(F32)
    conv_sum = jnp.zeros_like(resid)
    kernel_rows = []
    for tap in range(taps):
        shifted = resid_pad[:, tap : tap + row_count]
        conv_sum = conv_sum + conv_kernel[tap][:, None] * shifted
        kernel_rows.append(jnp.sum(upstream * shifted, axis=1))
    block_out = (resid + conv_sum).astype(BF16)
    kernel_part = jnp.stack(kernel_rows)

    grads = jnp.concatenate([dq, dkv], axis=1)
    if stride == 2:
        grads = to_rows(grads)
    grad_packed = (
        grads.reshape(heads, 3, HEAD_DIM, row_count).transpose(1, 0, 2, 3).reshape(3 * head_cols, row_count)
    )
    qkv_part = jnp.einsum("ct,dt->cd", grad_packed, normed, preferred_element_type=F32)
    grad_normed = jnp.einsum("cd,ct->dt", qkv_rows, grad_packed, preferred_element_type=F32)
    average = lax.psum(
        jnp.sum(inputs * grad_normed * norm_gain[:, None], axis=0, keepdims=True), "mp"
    ) / width
    grad_own = lax.psum_scatter(
        grad_normed.astype(BF16), "mp", scatter_dimension=0, tiled=True
    ).astype(F32)
    start = lax.axis_index("mp") * own_width
    gain_own = lax.dynamic_slice_in_dim(norm_gain, start, own_width, 0)
    own = frames.astype(F32)
    norm_term = inverse * (grad_own * gain_own[:, None]) - own * inverse**3 * average
    grad_frames = (back_sum + norm_term).astype(BF16)
    gain_part = jnp.sum(grad_own * own * inverse, axis=1)
    return (
        block_out,
        grad_frames,
        lax.psum(gain_part, "tm"),
        lax.psum(qkv_part.astype(BF16), "tm").astype(F32).reshape(3, head_cols, width),
        lax.psum(out_proj_part.astype(BF16), "tm").astype(F32),
        lax.psum(kernel_part, "tm"),
    )


def solution(mesh):
    return jax.shard_map(
        shards,
        mesh=mesh,
        in_specs=(
            P("mp", "tm"),
            P(),
            P(None, "mp", None),
            P("mp", None),
            P(None, "mp"),
            P("mp", "tm"),
        ),
        out_specs=(
            P("mp", "tm"),
            P("mp", "tm"),
            P("mp"),
            P(None, "mp", None),
            P("mp", None),
            P(None, "mp"),
        ),
        check_vma=False,
    )
```

```python
import functools

import jax
import jax.numpy as jnp
from jax import lax
from jax.experimental import pallas as pl
from jax.experimental.pallas import tpu as pltpu
from jax.sharding import PartitionSpec as P

HEAD_DIM = 64
VMEM_LIMIT = 52 * 1024 * 1024
F32 = jnp.float32
BF16 = jnp.bfloat16


def dot(a, b):
    return jnp.dot(a, b, preferred_element_type=F32)


def greet(n, stride):
    tm = lax.axis_index("tm")
    lane, me = tm % stride, tm // stride
    barrier = pltpu.get_barrier_semaphore()
    for k in range(1, n):
        peer = ((me + k) % n) * stride + lane
        pl.semaphore_signal(
            barrier, inc=1, device_id={"tm": peer}, device_id_type=pl.DeviceIdType.MESH
        )
    pl.semaphore_wait(barrier, n - 1)
    return lane, me


def attend_kernel(n, stride, q_ref, kv_ref, o_ref, lse_ref, all_ref, m_ref, l_ref, acc_ref, send_sem, recv_sem):
    heads, _, rows = q_ref.shape
    chunk = min(512, rows)
    lane, me = greet(n, stride)

    def pass_on(slot, h, way, target):
        return pltpu.make_async_remote_copy(
            src_ref=all_ref.at[slot, h],
            dst_ref=all_ref.at[slot, h],
            send_sem=send_sem.at[way, slot, h],
            recv_sem=recv_sem.at[slot, h],
            device_id={"tm": target * stride + lane},
            device_id_type=pl.DeviceIdType.MESH,
        )

    all_ref[me] = kv_ref[...]
    for h in range(heads):

        @pl.when(me + 1 < n)
        def _():
            pass_on(me, h, 1, me + 1).start()

        @pl.when(me > 0)
        def _():
            pass_on(me, h, 0, me - 1).start()

    m_ref[...] = jnp.full(m_ref.shape, -1e30, F32)
    l_ref[...] = jnp.zeros(l_ref.shape, F32)
    acc_ref[...] = jnp.zeros(acc_ref.shape, F32)

    def visit(slot, h):
        q = q_ref[h]
        q_pad = jnp.concatenate([q, jnp.zeros_like(q)], axis=0)
        for c in range(rows // chunk):
            kv_t = all_ref[slot, h, :, c * chunk : (c + 1) * chunk]
            scores = dot(kv_t.T, q_pad)
            old = m_ref[h]
            new = jnp.maximum(old, jnp.max(scores, axis=0, keepdims=True))
            weights = jnp.exp(scores - new)
            factor = jnp.exp(old - new)
            m_ref[h] = new
            l_ref[h] = l_ref[h] * factor + jnp.sum(weights, axis=0, keepdims=True)
            acc_ref[h] = acc_ref[h] * factor + dot(kv_t[HEAD_DIM:], weights.astype(BF16))

    def step(i, carry):
        turn, h = i // heads, i % heads
        side = 1 - 2 * (turn % 2)
        slot = me + side * ((turn + 1) // 2)

        @pl.when((slot >= 0) & (slot < n))
        def _():
            onward = me - side

            @pl.when(turn > 0)
            def _():
                pass_on(slot, h, 0, me + side).wait_recv()

            @pl.when((turn > 0) & (onward >= 0) & (onward < n))
            def _():
                pass_on(slot, h, turn % 2, onward).start()

            visit(slot, h)

        return carry

    lax.fori_loop(0, (2 * n - 1) * heads, step, 0)
    o_ref[...] = (acc_ref[...] / l_ref[...]).astype(BF16)
    lse_ref[...] = m_ref[...] + jnp.log(l_ref[...])

    def drain(i, carry):
        slot, h = i // heads, i % heads

        @pl.when((slot <= me) & (me + 1 < n))
        def _():
            pass_on(slot, h, 1, me + 1).wait_send()

        @pl.when((slot >= me) & (me > 0))
        def _():
            pass_on(slot, h, 0, me - 1).wait_send()

        return carry

    lax.fori_loop(0, n * heads, drain, 0)


def attend(n, stride, q, kv):
    heads, _, rows = q.shape
    vmem = pl.BlockSpec(memory_space=pltpu.VMEM)
    work = n * heads * rows * rows
    return pl.pallas_call(
        functools.partial(attend_kernel, n, stride),
        out_shape=(
            jax.ShapeDtypeStruct(q.shape, BF16),
            jax.ShapeDtypeStruct((heads, 1, rows), F32),
            jax.ShapeDtypeStruct((n, *kv.shape), BF16),
        ),
        in_specs=[vmem] * 2,
        out_specs=(vmem,) * 3,
        scratch_shapes=[
            pltpu.VMEM((heads, 1, rows), F32),
            pltpu.VMEM((heads, 1, rows), F32),
            pltpu.VMEM((heads, HEAD_DIM, rows), F32),
            pltpu.SemaphoreType.DMA((2, n, heads)),
            pltpu.SemaphoreType.DMA((n, heads)),
        ],
        cost_estimate=pl.CostEstimate(flops=work * 4 * HEAD_DIM, bytes_accessed=8 * kv.size * n, transcendentals=work),
        compiler_params=pltpu.CompilerParams(collective_id=0, has_side_effects=True, vmem_limit_bytes=VMEM_LIMIT),
        name="attend",
    )(q, kv)


def attend_grad_kernel(
    n, stride, q_ref, all_ref, up_ref, lse_ref, off_ref,
    dq_ref, dkv_ref, q_pad, up_pad, q_rows, up_rows, dq_acc, own, out_buf, in_buf, send_sem, recv_sem,
):
    heads, _, rows = q_ref.shape
    chunk = min(512, rows)
    lane, me = greet(n, stride)
    dq_acc[...] = jnp.zeros(dq_acc.shape, F32)

    def prepare(h, carry):
        q, up = q_ref[h], up_ref[h]
        blank = jnp.zeros_like(q)
        low, high = jnp.concatenate([q, blank], axis=0), jnp.concatenate([blank, up], axis=0)
        q_pad[h] = low
        up_pad[h] = high
        q_rows[h] = low.T
        up_rows[h] = high.T
        return carry

    lax.fori_loop(0, heads, prepare, 0)

    def visit(slot, h, store):
        for c in range(rows // chunk):
            kv_t = all_ref[slot, h, :, c * chunk : (c + 1) * chunk]
            kv = kv_t.T
            probs = jnp.exp(dot(kv, q_pad[h]) - lse_ref[h])
            grads = (probs * (dot(kv, up_pad[h]) - off_ref[h])).astype(BF16)
            dq_acc[h] = dq_acc[h] + dot(kv_t[:HEAD_DIM], grads)
            store(c, dot(grads, q_rows[h]) + dot(probs.astype(BF16), up_rows[h]))

    def pass_on(slot, h, way, target):
        return pltpu.make_async_remote_copy(
            src_ref=out_buf.at[slot, h],
            dst_ref=in_buf.at[way, slot, h],
            send_sem=send_sem.at[slot, h],
            recv_sem=recv_sem.at[way, slot, h],
            device_id={"tm": target * stride + lane},
            device_id_type=pl.DeviceIdType.MESH,
        )

    def far(i, carry):
        turn, h = i // heads, i % heads
        side = 1 - 2 * (turn % 2)
        slot = me + side * (n - 1 - turn // 2)
        way = 1 - turn % 2
        behind = me - side

        @pl.when((slot >= 0) & (slot < n))
        def _():
            joined = (behind >= 0) & (behind < n)

            def store(c, block):
                part = pl.ds(c * chunk, chunk)

                @pl.when(joined)
                def _():
                    if c == 0:
                        pass_on(slot, h, way, behind).wait_recv()
                    out_buf[slot, h, part, :] = (block + in_buf[way, slot, h, part, :].astype(F32)).astype(BF16)

                @pl.when(jnp.logical_not(joined))
                def _():
                    out_buf[slot, h, part, :] = block.astype(BF16)

            visit(slot, h, store)
            pass_on(slot, h, way, me + side).start()

        return carry

    lax.fori_loop(0, 2 * (n - 1) * heads, far, 0)

    def near(h, carry):
        def store(c, block):
            own[h, c * chunk : (c + 1) * chunk, :] = block

        visit(me, h, store)
        return carry

    lax.fori_loop(0, heads, near, 0)
    dq_ref[...] = (dq_acc[...] * HEAD_DIM ** (-0.5)).astype(BF16)

    def finish(h, carry):
        @pl.when(me + 1 < n)
        def _():
            pass_on(me, h, 0, me + 1).wait_recv()
            own[h] = own[h] + in_buf[0, me, h].astype(F32)

        @pl.when(me > 0)
        def _():
            pass_on(me, h, 1, me - 1).wait_recv()
            own[h] = own[h] + in_buf[1, me, h].astype(F32)

        dkv_ref[h] = own[h].T.astype(BF16)
        return carry

    lax.fori_loop(0, heads, finish, 0)

    def drain(i, carry):
        slot, h = i // heads, i % heads

        @pl.when(slot < me)
        def _():
            pass_on(slot, h, 0, me - 1).wait_send()

        @pl.when(slot > me)
        def _():
            pass_on(slot, h, 1, me + 1).wait_send()

        return carry

    lax.fori_loop(0, n * heads, drain, 0)


def attend_grad(n, stride, q, kv_all, up, lse, off):
    heads, _, rows = q.shape
    vmem = pl.BlockSpec(memory_space=pltpu.VMEM)
    work = n * heads * rows * rows
    wide = 2 * HEAD_DIM
    return pl.pallas_call(
        functools.partial(attend_grad_kernel, n, stride),
        out_shape=(
            jax.ShapeDtypeStruct(q.shape, BF16),
            jax.ShapeDtypeStruct((heads, wide, rows), BF16),
        ),
        in_specs=[vmem] * 5,
        out_specs=(vmem,) * 2,
        scratch_shapes=[
            pltpu.VMEM((heads, wide, rows), BF16),
            pltpu.VMEM((heads, wide, rows), BF16),
            pltpu.VMEM((heads, rows, wide), BF16),
            pltpu.VMEM((heads, rows, wide), BF16),
            pltpu.VMEM((heads, HEAD_DIM, rows), F32),
            pltpu.VMEM((heads, rows, wide), F32),
            pltpu.VMEM((n, heads, rows, wide), BF16),
            pltpu.VMEM((2, n, heads, rows, wide), BF16),
            pltpu.SemaphoreType.DMA((n, heads)),
            pltpu.SemaphoreType.DMA((2, n, heads)),
        ],
        cost_estimate=pl.CostEstimate(flops=work * 10 * HEAD_DIM, bytes_accessed=8 * kv_all.size, transcendentals=work),
        compiler_params=pltpu.CompilerParams(collective_id=1, has_side_effects=True, vmem_limit_bytes=VMEM_LIMIT),
        name="attend_grad",
    )(q, kv_all, up, lse, off)


def greet_all(axis, n):
    me = lax.axis_index(axis)
    barrier = pltpu.get_barrier_semaphore()
    for k in range(1, n):
        pl.semaphore_signal(
            barrier, inc=1, device_id={axis: (me + k) % n}, device_id_type=pl.DeviceIdType.MESH
        )
    pl.semaphore_wait(barrier, n - 1)
    return me


def scatter_sum_kernel(n, part_ref, row_ref, sum_ref, row_sum_ref, in_buf, in_rows, send_sem, recv_sem):
    me = greet_all("mp", n)
    copies = []
    for k in range(1, n):
        peer = (me + k) % n
        for which, (src, dst) in enumerate(
            ((part_ref.at[peer], in_buf.at[k - 1]), (row_ref, in_rows.at[k - 1]))
        ):
            copy = pltpu.make_async_remote_copy(
                src_ref=src,
                dst_ref=dst,
                send_sem=send_sem.at[which, k - 1],
                recv_sem=recv_sem.at[which, k - 1],
                device_id={"mp": peer},
                device_id_type=pl.DeviceIdType.MESH,
            )
            copy.start()
            copies.append(copy)
    for copy in copies:
        copy.wait()
    total, row = part_ref[me].astype(F32), row_ref[...]
    for k in range(1, n):
        total = total + in_buf[k - 1].astype(F32)
        row = row + in_rows[k - 1]
    sum_ref[...] = total
    row_sum_ref[...] = row


def scatter_sum(parts, row):
    n = parts.shape[0]
    vmem = pl.BlockSpec(memory_space=pltpu.VMEM)
    return pl.pallas_call(
        functools.partial(scatter_sum_kernel, n),
        out_shape=(jax.ShapeDtypeStruct(parts.shape[1:], F32), jax.ShapeDtypeStruct(row.shape, F32)),
        in_specs=[vmem] * 2,
        out_specs=(vmem,) * 2,
        scratch_shapes=[
            pltpu.VMEM((n - 1, *parts.shape[1:]), BF16),
            pltpu.VMEM((n - 1, *row.shape), F32),
            pltpu.SemaphoreType.DMA((2, n - 1)),
            pltpu.SemaphoreType.DMA((2, n - 1)),
        ],
        cost_estimate=pl.CostEstimate(flops=parts.size, bytes_accessed=20 * parts.size, transcendentals=0),
        compiler_params=pltpu.CompilerParams(collective_id=2, has_side_effects=True, vmem_limit_bytes=VMEM_LIMIT),
        name="scatter_sum",
    )(parts, row)


def small_sum_kernel(n, part_ref, sum_ref, in_buf, send_sem, recv_sem):
    me = greet_all("tm", n)
    copies = []
    for k in range(1, n):
        copy = pltpu.make_async_remote_copy(
            src_ref=part_ref,
            dst_ref=in_buf.at[me],
            send_sem=send_sem.at[k - 1],
            recv_sem=recv_sem.at[k - 1],
            device_id={"tm": (me + k) % n},
            device_id_type=pl.DeviceIdType.MESH,
        )
        copy.start()
        copies.append(copy)
    in_buf[me] = part_ref[...]
    for k in range(1, n):
        pltpu.make_async_remote_copy(
            src_ref=part_ref,
            dst_ref=in_buf.at[(me + n - k) % n],
            send_sem=send_sem.at[k - 1],
            recv_sem=recv_sem.at[k - 1],
            device_id={"tm": (me + n - k) % n},
            device_id_type=pl.DeviceIdType.MESH,
        ).wait()
    total = in_buf[0]
    for k in range(1, n):
        total = total + in_buf[k]
    sum_ref[...] = total


def small_sum(part):
    n = lax.axis_size("tm")
    vmem = pl.BlockSpec(memory_space=pltpu.VMEM)
    return pl.pallas_call(
        functools.partial(small_sum_kernel, n),
        out_shape=jax.ShapeDtypeStruct(part.shape, F32),
        in_specs=[vmem],
        out_specs=vmem,
        scratch_shapes=[
            pltpu.VMEM((n, *part.shape), F32),
            pltpu.SemaphoreType.DMA((n - 1,)),
            pltpu.SemaphoreType.DMA((n - 1,)),
        ],
        cost_estimate=pl.CostEstimate(flops=n * part.size, bytes_accessed=40 * n * part.size, transcendentals=0),
        compiler_params=pltpu.CompilerParams(collective_id=3, has_side_effects=True),
        name="small_sum",
    )(part)


def swap(block):
    count = lax.axis_size("tm")
    return lax.ppermute(block, "tm", [(i, i ^ 1) for i in range(count)])


def halves(block):
    low, high = jnp.split(block, 2, axis=0)
    odd = lax.axis_index("tm") % 2 == 1
    return jnp.where(odd, high, low), jnp.where(odd, low, high)


def to_heads(block):
    keep, give = halves(block)
    return jnp.concatenate([keep, swap(give)], axis=2)


def to_rows(block):
    keep, give = jnp.split(block, 2, axis=2)
    got = swap(give)
    odd = lax.axis_index("tm") % 2 == 1
    return jnp.concatenate([jnp.where(odd, got, keep), jnp.where(odd, keep, got)], axis=0)


def with_halo(cells, width):
    count = lax.axis_size("tm")
    ends = count - 1
    return jnp.concatenate(
        [
            lax.ppermute(cells[:, -width:], "tm", [(i, i + 1) for i in range(ends)]),
            cells,
            lax.ppermute(cells[:, :width], "tm", [(i + 1, i) for i in range(ends)]),
        ],
        axis=1,
    )


def shards(frames, norm_gain, w_qkv, w_out, conv_kernel, grad_out):
    own_width, row_count = frames.shape
    head_cols, width = w_qkv.shape[1:]
    heads = head_cols // HEAD_DIM
    tm = lax.axis_size("tm")
    stride = 2 if heads % 2 == 0 and tm % 2 == 0 else 1
    n = tm // stride
    taps = conv_kernel.shape[0]
    half = taps // 2

    upstream = grad_out.astype(F32)
    upstream_pad = with_halo(grad_out, half).astype(F32)
    back_sum = upstream
    for tap in range(taps):
        mirror = 2 * half - tap
        back_sum = back_sum + conv_kernel[tap][:, None] * upstream_pad[:, mirror : mirror + row_count]
    back_cast = back_sum.astype(BF16)

    gathered = lax.all_gather(frames, "mp", axis=0, tiled=True)
    inputs = gathered.astype(F32)
    inverse = lax.rsqrt(jnp.mean(inputs * inputs, axis=0, keepdims=True) + 1e-06)
    normed = (inputs * inverse * norm_gain[:, None]).astype(BF16)
    qkv_rows = w_qkv.reshape(3 * head_cols, width)
    packed = dot(qkv_rows, normed).astype(BF16).reshape(3, heads, HEAD_DIM, row_count)
    merged = packed.transpose(1, 0, 2, 3).reshape(heads, 3 * HEAD_DIM, row_count)
    if stride == 2:
        merged = to_heads(merged)
    q = merged[:, :HEAD_DIM] * jnp.asarray(HEAD_DIM ** (-0.5), BF16)
    attended_heads, lse, kv_all = attend(n, stride, q, merged[:, HEAD_DIM:])
    back_full = lax.all_gather(back_cast, "mp", axis=0, tiled=True)
    grad_attn = dot(w_out, back_full).astype(BF16).reshape(heads, HEAD_DIM, row_count)
    if stride == 2:
        attended = to_rows(attended_heads)
        up = to_heads(grad_attn)
    else:
        attended, up = attended_heads, grad_attn
    off = jnp.sum(up.astype(F32) * attended_heads.astype(F32), axis=1, keepdims=True)
    dq, dkv = attend_grad(n, stride, q, kv_all, up, lse, off)

    attn = attended.reshape(head_cols, row_count)
    out_proj_part = jnp.einsum("ct,dt->cd", attn, back_full, preferred_element_type=F32)
    out_proj_sum = lax.psum(out_proj_part.astype(BF16), "tm")
    dq, dkv, out_proj_sum = lax.optimization_barrier((dq, dkv, out_proj_sum))
    projected = jnp.einsum("cd,ct->dt", w_out, attn, preferred_element_type=F32)
    mixed = lax.psum_scatter(projected.astype(BF16), "mp", scatter_dimension=0, tiled=True)
    residual_sum = (frames.astype(F32) + mixed.astype(F32)).astype(BF16)
    resid_pad = with_halo(residual_sum, half).astype(F32)
    resid = residual_sum.astype(F32)
    conv_sum = jnp.zeros_like(resid)
    kernel_rows = []
    for tap in range(taps):
        shifted = resid_pad[:, tap : tap + row_count]
        conv_sum = conv_sum + conv_kernel[tap][:, None] * shifted
        kernel_rows.append(jnp.sum(upstream * shifted, axis=1))
    block_out = (resid + conv_sum).astype(BF16)
    kernel_part = jnp.stack(kernel_rows)

    grads = jnp.concatenate([dq, dkv], axis=1)
    if stride == 2:
        grads = to_rows(grads)
    grad_packed = (
        grads.reshape(heads, 3, HEAD_DIM, row_count).transpose(1, 0, 2, 3).reshape(3 * head_cols, row_count)
    )
    qkv_part = jnp.einsum("ct,dt->cd", grad_packed, normed, preferred_element_type=F32)
    grad_normed = jnp.einsum("cd,ct->dt", qkv_rows, grad_packed, preferred_element_type=F32)
    average_part = jnp.sum(inputs * grad_normed * norm_gain[:, None], axis=0, keepdims=True) / width
    grad_own, average = scatter_sum(
        grad_normed.astype(BF16).reshape(-1, own_width, row_count),
        jnp.broadcast_to(average_part, (8, row_count)),
    )
    average = average[:1]
    start = lax.axis_index("mp") * own_width
    gain_own = lax.dynamic_slice_in_dim(norm_gain, start, own_width, 0)
    own = frames.astype(F32)
    norm_term = inverse * (grad_own * gain_own[:, None]) - own * inverse**3 * average
    grad_frames = (back_sum + norm_term).astype(BF16)
    gain_part = jnp.sum(grad_own * own * inverse, axis=1)
    lines = jnp.concatenate([kernel_part, gain_part[None]])
    small = small_sum(jnp.pad(lines, ((0, -lines.shape[0] % 8), (0, 0))))
    return (
        block_out,
        grad_frames,
        small[taps],
        lax.psum(qkv_part.astype(BF16), "tm").astype(F32).reshape(3, head_cols, width),
        out_proj_sum.astype(F32),
        small[:taps],
    )


def solution(mesh):
    return jax.shard_map(
        shards,
        mesh=mesh,
        in_specs=(
            P("mp", "tm"),
            P(),
            P(None, "mp", None),
            P("mp", None),
            P(None, "mp"),
            P("mp", "tm"),
        ),
        out_specs=(
            P("mp", "tm"),
            P("mp", "tm"),
            P("mp"),
            P(None, "mp", None),
            P("mp", None),
            P(None, "mp"),
        ),
        check_vma=False,
    )
```

```python
import functools

import jax
import jax.numpy as jnp
from jax import lax
from jax.experimental import pallas as pl
from jax.experimental.pallas import tpu as pltpu
from jax.sharding import PartitionSpec as P

HEAD_DIM = 64
VMEM_LIMIT = 52 * 1024 * 1024
F32 = jnp.float32
BF16 = jnp.bfloat16


def dot(a, b):
    return jnp.dot(a, b, preferred_element_type=F32)


def greet(n, stride):
    tm = lax.axis_index("tm")
    lane, me = tm % stride, tm // stride
    barrier = pltpu.get_barrier_semaphore()
    for k in range(1, n):
        peer = ((me + k) % n) * stride + lane
        pl.semaphore_signal(
            barrier, inc=1, device_id={"tm": peer}, device_id_type=pl.DeviceIdType.MESH
        )
    pl.semaphore_wait(barrier, n - 1)
    return lane, me


def attend_kernel(n, stride, q_ref, kv_ref, o_ref, lse_ref, all_ref, m_ref, l_ref, acc_ref, send_sem, recv_sem):
    heads, _, rows = q_ref.shape
    chunk = min(512, rows)
    lane, me = greet(n, stride)

    def pass_on(slot, h, way, target):
        return pltpu.make_async_remote_copy(
            src_ref=all_ref.at[slot, h],
            dst_ref=all_ref.at[slot, h],
            send_sem=send_sem.at[way, slot, h],
            recv_sem=recv_sem.at[slot, h],
            device_id={"tm": target * stride + lane},
            device_id_type=pl.DeviceIdType.MESH,
        )

    all_ref[me] = kv_ref[...]
    for h in range(heads):

        @pl.when(me + 1 < n)
        def _():
            pass_on(me, h, 1, me + 1).start()

        @pl.when(me > 0)
        def _():
            pass_on(me, h, 0, me - 1).start()

    m_ref[...] = jnp.full(m_ref.shape, -1e30, F32)
    l_ref[...] = jnp.zeros(l_ref.shape, F32)
    acc_ref[...] = jnp.zeros(acc_ref.shape, F32)

    def visit(slot, h):
        q = q_ref[h]
        q_pad = jnp.concatenate([q, jnp.zeros_like(q)], axis=0)
        for c in range(rows // chunk):
            kv_t = all_ref[slot, h, :, c * chunk : (c + 1) * chunk]
            scores = dot(kv_t.T, q_pad)
            old = m_ref[h]
            new = jnp.maximum(old, jnp.max(scores, axis=0, keepdims=True))
            weights = jnp.exp(scores - new)
            factor = jnp.exp(old - new)
            m_ref[h] = new
            l_ref[h] = l_ref[h] * factor + jnp.sum(weights, axis=0, keepdims=True)
            acc_ref[h] = acc_ref[h] * factor + dot(kv_t[HEAD_DIM:], weights.astype(BF16))

    def step(i, carry):
        turn, h = i // heads, i % heads
        side = 1 - 2 * (turn % 2)
        slot = me + side * ((turn + 1) // 2)

        @pl.when((slot >= 0) & (slot < n))
        def _():
            onward = me - side

            @pl.when(turn > 0)
            def _():
                pass_on(slot, h, 0, me + side).wait_recv()

            @pl.when((turn > 0) & (onward >= 0) & (onward < n))
            def _():
                pass_on(slot, h, turn % 2, onward).start()

            visit(slot, h)

        return carry

    lax.fori_loop(0, (2 * n - 1) * heads, step, 0)
    o_ref[...] = (acc_ref[...] / l_ref[...]).astype(BF16)
    lse_ref[...] = m_ref[...] + jnp.log(l_ref[...])

    def drain(i, carry):
        slot, h = i // heads, i % heads

        @pl.when((slot <= me) & (me + 1 < n))
        def _():
            pass_on(slot, h, 1, me + 1).wait_send()

        @pl.when((slot >= me) & (me > 0))
        def _():
            pass_on(slot, h, 0, me - 1).wait_send()

        return carry

    lax.fori_loop(0, n * heads, drain, 0)


def attend(n, stride, q, kv):
    heads, _, rows = q.shape
    vmem = pl.BlockSpec(memory_space=pltpu.VMEM)
    work = n * heads * rows * rows
    return pl.pallas_call(
        functools.partial(attend_kernel, n, stride),
        out_shape=(
            jax.ShapeDtypeStruct(q.shape, BF16),
            jax.ShapeDtypeStruct((heads, 1, rows), F32),
            jax.ShapeDtypeStruct((n, *kv.shape), BF16),
        ),
        in_specs=[vmem] * 2,
        out_specs=(vmem,) * 3,
        scratch_shapes=[
            pltpu.VMEM((heads, 1, rows), F32),
            pltpu.VMEM((heads, 1, rows), F32),
            pltpu.VMEM((heads, HEAD_DIM, rows), F32),
            pltpu.SemaphoreType.DMA((2, n, heads)),
            pltpu.SemaphoreType.DMA((n, heads)),
        ],
        cost_estimate=pl.CostEstimate(flops=work * 4 * HEAD_DIM, bytes_accessed=8 * kv.size * n, transcendentals=work),
        compiler_params=pltpu.CompilerParams(collective_id=0, has_side_effects=True, vmem_limit_bytes=VMEM_LIMIT),
        name="attend",
    )(q, kv)


def attend_grad_kernel(
    n, stride, q_ref, all_ref, up_ref, lse_ref, off_ref,
    dq_ref, dkv_ref, q_pad, up_pad, q_rows, up_rows, dq_acc, own, out_buf, in_buf, send_sem, recv_sem,
):
    heads, _, rows = q_ref.shape
    chunk = min(512, rows)
    lane, me = greet(n, stride)
    dq_acc[...] = jnp.zeros(dq_acc.shape, F32)

    def prepare(h, carry):
        q, up = q_ref[h], up_ref[h]
        blank = jnp.zeros_like(q)
        low, high = jnp.concatenate([q, blank], axis=0), jnp.concatenate([blank, up], axis=0)
        q_pad[h] = low
        up_pad[h] = high
        q_rows[h] = low.T
        up_rows[h] = high.T
        return carry

    lax.fori_loop(0, heads, prepare, 0)

    def visit(slot, h, store):
        for c in range(rows // chunk):
            kv_t = all_ref[slot, h, :, c * chunk : (c + 1) * chunk]
            kv = kv_t.T
            probs = jnp.exp(dot(kv, q_pad[h]) - lse_ref[h])
            grads = (probs * (dot(kv, up_pad[h]) - off_ref[h])).astype(BF16)
            dq_acc[h] = dq_acc[h] + dot(kv_t[:HEAD_DIM], grads)
            store(c, dot(grads, q_rows[h]) + dot(probs.astype(BF16), up_rows[h]))

    def pass_on(slot, h, way, target):
        return pltpu.make_async_remote_copy(
            src_ref=out_buf.at[slot, h],
            dst_ref=in_buf.at[way, slot, h],
            send_sem=send_sem.at[slot, h],
            recv_sem=recv_sem.at[way, slot, h],
            device_id={"tm": target * stride + lane},
            device_id_type=pl.DeviceIdType.MESH,
        )

    def far(i, carry):
        turn, h = i // heads, i % heads
        side = 1 - 2 * (turn % 2)
        slot = me + side * (n - 1 - turn // 2)
        way = 1 - turn % 2
        behind = me - side

        @pl.when((slot >= 0) & (slot < n))
        def _():
            joined = (behind >= 0) & (behind < n)

            def store(c, block):
                part = pl.ds(c * chunk, chunk)

                @pl.when(joined)
                def _():
                    if c == 0:
                        pass_on(slot, h, way, behind).wait_recv()
                    out_buf[slot, h, part, :] = (block + in_buf[way, slot, h, part, :].astype(F32)).astype(BF16)

                @pl.when(jnp.logical_not(joined))
                def _():
                    out_buf[slot, h, part, :] = block.astype(BF16)

            visit(slot, h, store)
            pass_on(slot, h, way, me + side).start()

        return carry

    lax.fori_loop(0, 2 * (n - 1) * heads, far, 0)

    def near(h, carry):
        def store(c, block):
            own[h, c * chunk : (c + 1) * chunk, :] = block

        visit(me, h, store)
        return carry

    lax.fori_loop(0, heads, near, 0)
    dq_ref[...] = (dq_acc[...] * HEAD_DIM ** (-0.5)).astype(BF16)

    def finish(h, carry):
        @pl.when(me + 1 < n)
        def _():
            pass_on(me, h, 0, me + 1).wait_recv()
            own[h] = own[h] + in_buf[0, me, h].astype(F32)

        @pl.when(me > 0)
        def _():
            pass_on(me, h, 1, me - 1).wait_recv()
            own[h] = own[h] + in_buf[1, me, h].astype(F32)

        dkv_ref[h] = own[h].T.astype(BF16)
        return carry

    lax.fori_loop(0, heads, finish, 0)

    def drain(i, carry):
        slot, h = i // heads, i % heads

        @pl.when(slot < me)
        def _():
            pass_on(slot, h, 0, me - 1).wait_send()

        @pl.when(slot > me)
        def _():
            pass_on(slot, h, 1, me + 1).wait_send()

        return carry

    lax.fori_loop(0, n * heads, drain, 0)


def attend_grad(n, stride, q, kv_all, up, lse, off):
    heads, _, rows = q.shape
    vmem = pl.BlockSpec(memory_space=pltpu.VMEM)
    work = n * heads * rows * rows
    wide = 2 * HEAD_DIM
    return pl.pallas_call(
        functools.partial(attend_grad_kernel, n, stride),
        out_shape=(
            jax.ShapeDtypeStruct(q.shape, BF16),
            jax.ShapeDtypeStruct((heads, wide, rows), BF16),
        ),
        in_specs=[vmem] * 5,
        out_specs=(vmem,) * 2,
        scratch_shapes=[
            pltpu.VMEM((heads, wide, rows), BF16),
            pltpu.VMEM((heads, wide, rows), BF16),
            pltpu.VMEM((heads, rows, wide), BF16),
            pltpu.VMEM((heads, rows, wide), BF16),
            pltpu.VMEM((heads, HEAD_DIM, rows), F32),
            pltpu.VMEM((heads, rows, wide), F32),
            pltpu.VMEM((n, heads, rows, wide), BF16),
            pltpu.VMEM((2, n, heads, rows, wide), BF16),
            pltpu.SemaphoreType.DMA((n, heads)),
            pltpu.SemaphoreType.DMA((2, n, heads)),
        ],
        cost_estimate=pl.CostEstimate(flops=work * 10 * HEAD_DIM, bytes_accessed=8 * kv_all.size, transcendentals=work),
        compiler_params=pltpu.CompilerParams(collective_id=1, has_side_effects=True, vmem_limit_bytes=VMEM_LIMIT),
        name="attend_grad",
    )(q, kv_all, up, lse, off)


def greet_all(axis, n):
    me = lax.axis_index(axis)
    barrier = pltpu.get_barrier_semaphore()
    for k in range(1, n):
        pl.semaphore_signal(
            barrier, inc=1, device_id={axis: (me + k) % n}, device_id_type=pl.DeviceIdType.MESH
        )
    pl.semaphore_wait(barrier, n - 1)
    return me


def scatter_sum_kernel(n, part_ref, row_ref, sum_ref, row_sum_ref, in_buf, in_rows, send_sem, recv_sem):
    me = greet_all("mp", n)
    copies = []
    for k in range(1, n):
        peer = (me + k) % n
        for which, (src, dst) in enumerate(
            ((part_ref.at[peer], in_buf.at[k - 1]), (row_ref, in_rows.at[k - 1]))
        ):
            copy = pltpu.make_async_remote_copy(
                src_ref=src,
                dst_ref=dst,
                send_sem=send_sem.at[which, k - 1],
                recv_sem=recv_sem.at[which, k - 1],
                device_id={"mp": peer},
                device_id_type=pl.DeviceIdType.MESH,
            )
            copy.start()
            copies.append(copy)
    for copy in copies:
        copy.wait()
    total, row = part_ref[me].astype(F32), row_ref[...]
    for k in range(1, n):
        total = total + in_buf[k - 1].astype(F32)
        row = row + in_rows[k - 1]
    sum_ref[...] = total
    row_sum_ref[...] = row


def scatter_sum(parts, row):
    n = parts.shape[0]
    vmem = pl.BlockSpec(memory_space=pltpu.VMEM)
    return pl.pallas_call(
        functools.partial(scatter_sum_kernel, n),
        out_shape=(jax.ShapeDtypeStruct(parts.shape[1:], F32), jax.ShapeDtypeStruct(row.shape, F32)),
        in_specs=[vmem] * 2,
        out_specs=(vmem,) * 2,
        scratch_shapes=[
            pltpu.VMEM((n - 1, *parts.shape[1:]), BF16),
            pltpu.VMEM((n - 1, *row.shape), F32),
            pltpu.SemaphoreType.DMA((2, n - 1)),
            pltpu.SemaphoreType.DMA((2, n - 1)),
        ],
        cost_estimate=pl.CostEstimate(flops=parts.size, bytes_accessed=20 * parts.size, transcendentals=0),
        compiler_params=pltpu.CompilerParams(collective_id=2, has_side_effects=True, vmem_limit_bytes=VMEM_LIMIT),
        name="scatter_sum",
    )(parts, row)


def small_sum_kernel(n, part_ref, sum_ref, in_buf, send_sem, recv_sem):
    me = greet_all("tm", n)
    copies = []
    for k in range(1, n):
        copy = pltpu.make_async_remote_copy(
            src_ref=part_ref,
            dst_ref=in_buf.at[me],
            send_sem=send_sem.at[k - 1],
            recv_sem=recv_sem.at[k - 1],
            device_id={"tm": (me + k) % n},
            device_id_type=pl.DeviceIdType.MESH,
        )
        copy.start()
        copies.append(copy)
    in_buf[me] = part_ref[...]
    for k in range(1, n):
        pltpu.make_async_remote_copy(
            src_ref=part_ref,
            dst_ref=in_buf.at[(me + n - k) % n],
            send_sem=send_sem.at[k - 1],
            recv_sem=recv_sem.at[k - 1],
            device_id={"tm": (me + n - k) % n},
            device_id_type=pl.DeviceIdType.MESH,
        ).wait()
    total = in_buf[0]
    for k in range(1, n):
        total = total + in_buf[k]
    sum_ref[...] = total


def small_sum(part):
    n = lax.axis_size("tm")
    vmem = pl.BlockSpec(memory_space=pltpu.VMEM)
    return pl.pallas_call(
        functools.partial(small_sum_kernel, n),
        out_shape=jax.ShapeDtypeStruct(part.shape, F32),
        in_specs=[vmem],
        out_specs=vmem,
        scratch_shapes=[
            pltpu.VMEM((n, *part.shape), F32),
            pltpu.SemaphoreType.DMA((n - 1,)),
            pltpu.SemaphoreType.DMA((n - 1,)),
        ],
        cost_estimate=pl.CostEstimate(flops=n * part.size, bytes_accessed=40 * n * part.size, transcendentals=0),
        compiler_params=pltpu.CompilerParams(collective_id=3, has_side_effects=True),
        name="small_sum",
    )(part)


def swap(block):
    count = lax.axis_size("tm")
    return lax.ppermute(block, "tm", [(i, i ^ 1) for i in range(count)])


def halves(block):
    low, high = jnp.split(block, 2, axis=0)
    odd = lax.axis_index("tm") % 2 == 1
    return jnp.where(odd, high, low), jnp.where(odd, low, high)


def to_heads(block):
    keep, give = halves(block)
    return jnp.concatenate([keep, swap(give)], axis=2)


def to_rows(block):
    keep, give = jnp.split(block, 2, axis=2)
    got = swap(give)
    odd = lax.axis_index("tm") % 2 == 1
    return jnp.concatenate([jnp.where(odd, got, keep), jnp.where(odd, keep, got)], axis=0)


def with_halo(cells, width):
    count = lax.axis_size("tm")
    ends = count - 1
    return jnp.concatenate(
        [
            lax.ppermute(cells[:, -width:], "tm", [(i, i + 1) for i in range(ends)]),
            cells,
            lax.ppermute(cells[:, :width], "tm", [(i + 1, i) for i in range(ends)]),
        ],
        axis=1,
    )


def shards(frames, norm_gain, w_qkv, w_out, conv_kernel, grad_out):
    own_width, row_count = frames.shape
    head_cols, width = w_qkv.shape[1:]
    heads = head_cols // HEAD_DIM
    tm = lax.axis_size("tm")
    stride = 2 if heads % 2 == 0 and tm % 2 == 0 else 1
    n = tm // stride
    taps = conv_kernel.shape[0]
    half = taps // 2

    upstream = grad_out.astype(F32)
    upstream_pad = with_halo(grad_out, half).astype(F32)
    back_sum = upstream
    for tap in range(taps):
        mirror = 2 * half - tap
        back_sum = back_sum + conv_kernel[tap][:, None] * upstream_pad[:, mirror : mirror + row_count]
    back_cast = back_sum.astype(BF16)

    gathered = lax.all_gather(frames, "mp", axis=0, tiled=True)
    inputs = gathered.astype(F32)
    inverse = lax.rsqrt(jnp.mean(inputs * inputs, axis=0, keepdims=True) + 1e-06)
    normed = (inputs * inverse * norm_gain[:, None]).astype(BF16)
    qkv_rows = w_qkv.reshape(3 * head_cols, width)
    packed = dot(qkv_rows, normed).astype(BF16).reshape(3, heads, HEAD_DIM, row_count)
    merged = packed.transpose(1, 0, 2, 3).reshape(heads, 3 * HEAD_DIM, row_count)
    if stride == 2:
        merged = to_heads(merged)
    q = merged[:, :HEAD_DIM] * jnp.asarray(HEAD_DIM ** (-0.5), BF16)
    attended_heads, lse, kv_all = attend(n, stride, q, merged[:, HEAD_DIM:])
    back_full = lax.all_gather(back_cast, "mp", axis=0, tiled=True)
    grad_attn = dot(w_out, back_full).astype(BF16).reshape(heads, HEAD_DIM, row_count)
    if stride == 2:
        attended = to_rows(attended_heads)
        up = to_heads(grad_attn)
    else:
        attended, up = attended_heads, grad_attn
    off = jnp.sum(up.astype(F32) * attended_heads.astype(F32), axis=1, keepdims=True)
    dq, dkv = attend_grad(n, stride, q, kv_all, up, lse, off)

    attn = attended.reshape(head_cols, row_count)
    out_proj_part = jnp.einsum("ct,dt->cd", attn, back_full, preferred_element_type=F32)
    out_proj_sum = lax.psum(out_proj_part.astype(BF16), "tm")
    dq, dkv, out_proj_sum = lax.optimization_barrier((dq, dkv, out_proj_sum))
    projected = jnp.einsum("cd,ct->dt", w_out, attn, preferred_element_type=F32)
    mixed = lax.psum_scatter(projected.astype(BF16), "mp", scatter_dimension=0, tiled=True)
    residual_sum = (frames.astype(F32) + mixed.astype(F32)).astype(BF16)
    resid_pad = with_halo(residual_sum, half).astype(F32)
    resid = residual_sum.astype(F32)
    conv_sum = jnp.zeros_like(resid)
    kernel_rows = []
    for tap in range(taps):
        shifted = resid_pad[:, tap : tap + row_count]
        conv_sum = conv_sum + conv_kernel[tap][:, None] * shifted
        kernel_rows.append(jnp.sum(upstream * shifted, axis=1))
    block_out = (resid + conv_sum).astype(BF16)
    kernel_part = jnp.stack(kernel_rows)

    grads = jnp.concatenate([dq, dkv], axis=1)
    if stride == 2:
        grads = to_rows(grads)
    grad_packed = (
        grads.reshape(heads, 3, HEAD_DIM, row_count).transpose(1, 0, 2, 3).reshape(3 * head_cols, row_count)
    )
    qkv_part = jnp.einsum("ct,dt->cd", grad_packed, normed, preferred_element_type=F32)
    qkv_share = lax.psum_scatter(qkv_part.astype(BF16), "tm", scatter_dimension=0, tiled=True)
    qkv_sum = lax.all_gather(qkv_share, "tm", axis=0, tiled=True)
    grad_normed = jnp.einsum("cd,ct->dt", qkv_rows, grad_packed, preferred_element_type=F32)
    average_part = jnp.sum(inputs * grad_normed * norm_gain[:, None], axis=0, keepdims=True) / width
    grad_own, average = scatter_sum(
        grad_normed.astype(BF16).reshape(-1, own_width, row_count),
        jnp.broadcast_to(average_part, (8, row_count)),
    )
    average = average[:1]
    start = lax.axis_index("mp") * own_width
    gain_own = lax.dynamic_slice_in_dim(norm_gain, start, own_width, 0)
    own = frames.astype(F32)
    norm_term = inverse * (grad_own * gain_own[:, None]) - own * inverse**3 * average
    grad_frames = (back_sum + norm_term).astype(BF16)
    gain_part = jnp.sum(grad_own * own * inverse, axis=1)
    lines = jnp.concatenate([kernel_part, gain_part[None]])
    small = small_sum(jnp.pad(lines, ((0, -lines.shape[0] % 8), (0, 0))))
    return (
        block_out,
        grad_frames,
        small[taps],
        qkv_sum.astype(F32).reshape(3, head_cols, width),
        out_proj_sum.astype(F32),
        small[:taps],
    )


def solution(mesh):
    return jax.shard_map(
        shards,
        mesh=mesh,
        in_specs=(
            P("mp", "tm"),
            P(),
            P(None, "mp", None),
            P("mp", None),
            P(None, "mp"),
            P("mp", "tm"),
        ),
        out_specs=(
            P("mp", "tm"),
            P("mp", "tm"),
            P("mp"),
            P(None, "mp", None),
            P("mp", None),
            P(None, "mp"),
        ),
        check_vma=False,
    )
```
